32 devices in a mesh: dom: 8 (over z, x), rep: 4 (over y, core).
Axes of the slice: x: 2, y: 2, z: 4, core: 2. Of those that a mesh axis runs over, the one named last changes fastest.
Arguments:
- node_features: bfloat16 [4, 8192, 256], P('rep', 'dom'), may hold values from -32 to 32
- cotangent: bfloat16 [4, 8192, 256], P('rep', 'dom'), may hold values from -6 to 6
- w_qkv: bfloat16 [256, 768], replicated, may hold values from -0.375 to 0.375
- w_out: bfloat16 [256, 256], replicated, may hold values from -0.375 to 0.375
- w_up: bfloat16 [256, 512], replicated, may hold values from -0.375 to 0.375
- w_down: bfloat16 [512, 256], replicated, may hold values from -0.25 to 0.25
- tile_cols: int32 [4, 64, 8], P('rep'), may hold values from 0 to 63, as said below
- tile_count: int32 [4, 64], P('rep', 'dom'), may hold values from 1 to 9
- live: int32 [4, 8192], P('rep', 'dom'), may hold values 0 or 1
Outputs:
- layer_out: bfloat16 [4, 8192, 256], P('rep', 'dom')
- feature_grad: bfloat16 [4, 8192, 256], P('rep', 'dom')
- grad_qkv: float32 [256, 768], replicated
- grad_wout: float32 [256, 256], replicated
- grad_up: float32 [256, 512], replicated
- grad_down: float32 [512, 256], replicated
The draws below stay inside these ranges and needn't reach their ends.
Inputs may be any that keep to these rules, and one draw needn't show every extreme that they name: `tile_cols`: within each aligned run of 8 row blocks, the 64 listed blocks are all different; at most 8 of them lie in any one aligned run of 8 blocks, and exactly 8 lie in some such run.
All inputs are finite; a program needn't handle non-finite values. No bound on the sum of `live` on one device may be relied on, other than what follows from the above.
Results may differ from the reference program's by a relative error of at most 0.015.
Values may be sent and summed in bfloat16 or wider, within the bound.
A program may use at most 192 MiB of HBM per device.

```python
import math
import jax
import jax.numpy as jnp
from jax import lax

D = 256
HEADS = 8
F = 512
BLOCK = 128
EXP = 8
NB_DEV = 8
NBLK = 64
NODES = 8192
CAP = 8
N_DOM = 8
N_REP = 4


def draw_node_features(key, part):
    first = jax.random.fold_in(key, 0)
    shape = (N_REP, NODES, D)
    values = jnp.clip(jax.random.normal(first, shape, jnp.float32), -4.0, 4.0)
    return values.astype(jnp.bfloat16)


def draw_tile_cols(key, part):
    cells = N_DOM * CAP
    listed = NB_DEV * EXP

    def one_run(run_key):
        key_a, key_b, key_c, key_d = jax.random.split(run_key, 4)
        order = jax.random.permutation(key_a, cells).astype(jnp.int32)
        favoured = jax.random.randint(key_b, (), 0, N_DOM)
        cell_ids = jnp.arange(cells, dtype=jnp.int32)
        score = order + jnp.where(cell_ids // CAP == favoured, cells, 0)
        chosen = jnp.argsort(-score)[:listed]
        chosen = chosen[jax.random.permutation(key_c, listed)]
        peer = chosen // CAP
        slot = chosen % CAP
        offset = jax.random.randint(key_d, (N_DOM,), 0, NB_DEV)
        blocks = peer * NB_DEV + (offset[peer] + slot) % NB_DEV
        return blocks.reshape(NB_DEV, EXP)
    run_keys = jax.random.split(jax.random.fold_in(key, 11), N_REP * N_DOM)
    table = jax.vmap(one_run)(run_keys)
    return table.reshape(N_REP, N_DOM * NB_DEV, EXP).astype(jnp.int32)


def plant(entries, rng, low, high):
    dims = entries.shape
    place = [jax.random.randint(jax.random.fold_in(rng, axis), (), 0, dims[axis]) for axis in range(len(dims))]
    entries = entries.at[tuple(place)].set(low)
    longest = dims.index(max(dims))
    place[longest] = (place[longest] + 1) % dims[longest]
    return entries.at[tuple(place)].set(high)


def block_levels(key, shape, shards, smallest, high):
    factor_of = 1.0
    for dim, parts in shards:
        draws = jax.random.uniform(jax.random.fold_in(jax.random.fold_in(key, 6), dim), (parts,), jnp.float32, smallest / len(shards), high / len(shards))
        factor_of = factor_of * jnp.repeat(jnp.exp(draws), shape[dim] // parts).reshape((-1,) + (1,) * (len(shape) - 1 - dim))
    return factor_of


def scatter_about(key, extent, deviation, reach, cuts=(), kind=jnp.bfloat16):
    entries = deviation * jax.random.normal(key, extent, jnp.float32)
    if cuts:
        entries = entries * block_levels(key, extent, cuts, -0.22, 0.18)
    return jnp.clip(entries, -reach, reach).astype(kind)


def setup_inputs(seed: int = 0) -> dict:
    seeds = jax.random.split(jax.random.key(seed), 10)
    node_features = draw_node_features(jax.random.fold_in(seeds[9], 71), 0)
    cotangent = scatter_about(seeds[1], (N_REP, NODES, D), 1.0, 6.0, ((0, 4), (1, 8)))
    w_qkv = scatter_about(seeds[2], (D, 3 * D), D ** -0.5, 0.375)
    w_out = scatter_about(seeds[3], (D, D), D ** -0.5, 0.375)
    w_up = scatter_about(seeds[4], (D, F), D ** -0.5, 0.375)
    w_down = scatter_about(seeds[5], (F, D), F ** -0.5, 0.25)
    tile_cols = draw_tile_cols(jax.random.fold_in(seeds[9], 71), 0)
    tile_count = plant(jax.random.randint(seeds[7], (N_REP, NBLK), 1, EXP + 2), jax.random.fold_in(seeds[7], 1), 1, (EXP + 2) - 1).astype(jnp.int32)
    live = plant((jax.random.randint(seeds[8], (N_REP, NODES), 0, 8) < 7).astype(jnp.int32), jax.random.fold_in(seeds[8], 1), 0, 1)
    return dict(node_features=node_features, cotangent=cotangent, w_qkv=w_qkv, w_out=w_out, w_up=w_up, w_down=w_down, tile_cols=tile_cols, tile_count=tile_count, live=live)


NEG = -1.0e30


def split_heads(values):
    return values.reshape(values.shape[:-1] + (HEADS, values.shape[-1] // HEADS))


def allowed_keys(tile_ok, key_live, key_ids, query_ids):
    live_part = key_live[:, None, :, :] > 0.5
    self_part = key_ids[:, None, :, :] == query_ids[:, :, None, None]
    return tile_ok[:, None, :, None] & (live_part | self_part)


def probabilities(queries, keys, allowed, score_scale):
    scores = jnp.einsum("gqhd,gtkhd->ghqtk", split_heads(queries).astype(jnp.float32), split_heads(keys).astype(jnp.float32)) * score_scale
    scores = jnp.where(allowed[:, None], scores, NEG)
    largest = jnp.max(scores, axis=(3, 4), keepdims=True)
    weights = jnp.exp(scores - largest)
    total = jnp.sum(weights, axis=(3, 4), keepdims=True)
    return (weights / total).astype(jnp.bfloat16)


def attend_group(queries, kv_tiles, allowed, score_scale):
    width = queries.shape[-1]
    probs = probabilities(queries, kv_tiles[..., :width], allowed, score_scale)
    result = jnp.einsum("ghqtk,gtkhd->gqhd", probs.astype(jnp.float32), split_heads(kv_tiles[..., width:]).astype(jnp.float32))
    return result.reshape(queries.shape)


def back_group(queries, kv_tiles, allowed, d_attended, attended32, score_scale):
    width = queries.shape[-1]
    keys = kv_tiles[..., :width]
    values = kv_tiles[..., width:]
    probs = probabilities(queries, keys, allowed, score_scale)
    d_heads = split_heads(d_attended).astype(jnp.float32)
    delta = jnp.transpose(jnp.sum(d_heads * split_heads(attended32), axis=-1), (0, 2, 1))
    d_probs = jnp.einsum("gqhd,gtkhd->ghqtk", d_heads, split_heads(values).astype(jnp.float32))
    d_scores = (probs.astype(jnp.float32) * (d_probs - delta[:, :, :, None, None]) * score_scale).astype(jnp.bfloat16)
    d_queries = jnp.einsum("ghqtk,gtkhd->gqhd", d_scores.astype(jnp.float32), split_heads(keys).astype(jnp.float32))
    d_queries = d_queries.reshape(queries.shape).astype(jnp.bfloat16)
    d_keys = jnp.einsum("ghqtk,gqhd->gtkhd", d_scores.astype(jnp.float32), split_heads(queries).astype(jnp.float32))
    d_values = jnp.einsum("ghqtk,gqhd->gtkhd", probs.astype(jnp.float32), d_heads)
    merged_shape = d_keys.shape[:3] + (width,)
    d_kv = jnp.concatenate([d_keys.reshape(merged_shape), d_values.reshape(merged_shape)], axis=-1)
    return d_queries, d_kv[:, 0], d_kv[:, 1:]


def reference(node_features, cotangent, w_qkv, w_out, w_up, w_down, tile_cols, tile_count, live):
    width = node_features.shape[2]
    nodes = node_features.shape[1]
    block_total = nodes // BLOCK
    group_size = math.gcd(block_total, 4)
    group_count = block_total // group_size
    score_scale = float(width // HEADS) ** -0.5
    outputs = []
    feature_grads = []
    grad_qkv = jnp.zeros((width, 3 * width), jnp.float32)
    grad_wout = jnp.zeros((width, width), jnp.float32)
    grad_up = jnp.zeros((width, w_up.shape[1]), jnp.float32)
    grad_down = jnp.zeros((w_up.shape[1], width), jnp.float32)
    row_ids = jnp.arange(BLOCK, dtype=jnp.int32)
    block_ids = jnp.arange(block_total, dtype=jnp.int32)
    for slab in range(N_REP):
        features = node_features[slab]
        grad_in = cotangent[slab]
        qkv_rows = jnp.dot(features, w_qkv, preferred_element_type=jnp.float32).astype(jnp.bfloat16)
        queries = qkv_rows[:, :width].reshape(block_total, BLOCK, width)
        kv_rows = qkv_rows[:, width:].reshape(block_total, BLOCK, 2 * width)
        live_rows = live[slab].astype(jnp.float32).reshape(block_total, BLOCK)
        tile_ids = jnp.concatenate([block_ids[:, None], tile_cols[slab].astype(jnp.int32)], axis=1)
        tile_ok = jnp.concatenate([jnp.ones((block_total, 1), bool), jnp.arange(EXP, dtype=jnp.int32)[None, :] < tile_count[slab].astype(jnp.int32)[:, None] - 1], axis=1)
        query_ids = block_ids[:, None] * BLOCK + row_ids[None, :]

        def gather_group(index):
            start = (index * group_size).astype(jnp.int32)
            group_tiles = lax.dynamic_slice_in_dim(tile_ids, start, group_size, 0)
            group_queries = lax.dynamic_slice_in_dim(queries, start, group_size, 0)
            group_kv = kv_rows[group_tiles]
            key_ids = group_tiles[:, :, None] * BLOCK + row_ids[None, None, :]
            allowed = allowed_keys(lax.dynamic_slice_in_dim(tile_ok, start, group_size, 0), live_rows[group_tiles], key_ids, lax.dynamic_slice_in_dim(query_ids, start, group_size, 0))
            return group_tiles, group_queries, group_kv, allowed, start

        def forward_one(index):
            group_tiles, group_queries, group_kv, allowed, start = gather_group(index)
            return attend_group(group_queries, group_kv, allowed, score_scale)

        attended32 = lax.map(forward_one, jnp.arange(group_count, dtype=jnp.int32)).reshape(nodes, width)
        attended = attended32.astype(jnp.bfloat16)
        mixed = (features.astype(jnp.float32) + jnp.dot(attended, w_out, preferred_element_type=jnp.float32)).astype(jnp.bfloat16)
        pre = jnp.dot(mixed, w_up, preferred_element_type=jnp.float32)
        act = jax.nn.silu(pre).astype(jnp.bfloat16)
        outputs.append((mixed.astype(jnp.float32) + jnp.dot(act, w_down, preferred_element_type=jnp.float32)).astype(jnp.bfloat16))
        sigma = jax.nn.sigmoid(pre)
        d_act = (jnp.dot(grad_in, w_down.T, preferred_element_type=jnp.float32) * sigma * (1.0 + pre * (1.0 - sigma))).astype(jnp.bfloat16)
        d_mixed = (grad_in.astype(jnp.float32) + jnp.dot(d_act, w_up.T, preferred_element_type=jnp.float32)).astype(jnp.bfloat16)
        d_attended = jnp.dot(d_mixed, w_out.T, preferred_element_type=jnp.float32).astype(jnp.bfloat16)
        d_att_blocks = d_attended.reshape(block_total, BLOCK, width)
        att_blocks = attended32.reshape(block_total, BLOCK, width)

        def back_step(accumulated, index):
            group_tiles, group_queries, group_kv, allowed, start = gather_group(index)
            d_queries, near_term, far_term = back_group(group_queries, group_kv, allowed, lax.dynamic_slice_in_dim(d_att_blocks, start, group_size, 0), lax.dynamic_slice_in_dim(att_blocks, start, group_size, 0), score_scale)
            accumulated = accumulated.at[group_tiles[:, 0]].add(near_term)
            rounded = lax.optimization_barrier(far_term.astype(jnp.bfloat16)).astype(jnp.float32)
            accumulated = accumulated.at[group_tiles[:, 1:]].add(rounded)
            return accumulated, d_queries

        accumulated, d_queries = lax.scan(back_step, jnp.zeros((block_total, BLOCK, 2 * width), jnp.float32), jnp.arange(group_count, dtype=jnp.int32))
        d_kv = accumulated.reshape(nodes, 2 * width).astype(jnp.bfloat16)
        d_qkv = jnp.concatenate([d_queries.reshape(nodes, width), d_kv], axis=1)
        feature_grads.append((d_mixed.astype(jnp.float32) + jnp.dot(d_qkv, w_qkv.T, preferred_element_type=jnp.float32)).astype(jnp.bfloat16))
        grad_qkv = grad_qkv + jnp.dot(features.T, d_qkv, preferred_element_type=jnp.float32)
        grad_wout = grad_wout + jnp.dot(attended.T, d_mixed, preferred_element_type=jnp.float32)
        grad_up = grad_up + jnp.dot(mixed.T, d_act, preferred_element_type=jnp.float32)
        grad_down = grad_down + jnp.dot(act.T, grad_in, preferred_element_type=jnp.float32)
    factor = float(nodes * N_REP) ** -0.5
    return (jnp.stack(outputs), jnp.stack(feature_grads), grad_qkv * factor, grad_wout * factor, grad_up * factor, grad_down * factor)
```

```python
import math

import jax
import jax.numpy as jnp
from jax import lax
from jax.experimental import pallas as pl
from jax.experimental.pallas import tpu as pltpu
from jax.sharding import PartitionSpec as P

HEADS = 8
BLOCK = 128
EXP = 8
TILES = EXP + 1
EXTRA = 16
PAIRS = HEADS // 2

F32 = jnp.float32
BF16 = jnp.bfloat16


def dot_nn(a, b):
    return lax.dot_general(a, b, (((1,), (0,)), ((), ())), preferred_element_type=F32)


def dot_nt(a, b):
    return lax.dot_general(a, b, (((1,), (1,)), ((), ())), preferred_element_type=F32)


def dot_tn(a, b):
    return lax.dot_general(a, b, (((0,), (0,)), ((), ())), preferred_element_type=F32)


def layer_kernel(
    row_s, slot_s, self_s, count_s,
    feat_ref, cot_ref, live_ref, gath_ref, glive_ref,
    wqkv_ref, wqkvt_ref, wout_ref, wup_ref, wdown_ref,
    out_ref, part_ref, near_ref, far_ref, gqkv_ref, gout_ref, gup_ref, gdown_ref,
    feat_s, k_s, v_s, kt_s, vt_s, bias_s, e_s, ds_s, qbd_s, dobd_s, att_s, dq_s, rl_s,
):
    b = pl.program_id(0)
    width = feat_ref.shape[1]
    hw = width // HEADS
    scale = float(hw) ** -0.5

    @pl.when(b == 0)
    def _():
        gqkv_ref[...] = jnp.zeros_like(gqkv_ref)
        gout_ref[...] = jnp.zeros_like(gout_ref)
        gup_ref[...] = jnp.zeros_like(gup_ref)
        gdown_ref[...] = jnp.zeros_like(gdown_ref)

    eye = (
        lax.broadcasted_iota(jnp.int32, (BLOCK, BLOCK), 0)
        == lax.broadcasted_iota(jnp.int32, (BLOCK, BLOCK), 1)
    ).astype(F32)
    feat = feat_ref[...]
    cot = cot_ref[...]
    feat_s[0:BLOCK, :] = feat
    bias_s[0:BLOCK, :] = (jnp.maximum(live_ref[...], eye) - 1.0) * 1e30
    for t in range(EXP):
        row = pl.multiple_of(row_s[b * EXP + t], 16)
        place = pl.multiple_of(slot_s[b * EXP + t] * BLOCK, BLOCK)
        active = (t + 1 < count_s[b]).astype(F32)
        mine = self_s[b * EXP + t].astype(F32)
        feat_s[(t + 1) * BLOCK:(t + 2) * BLOCK, :] = gath_ref[pl.ds(row, BLOCK), :]
        seen = jnp.maximum(glive_ref[pl.ds(place, BLOCK), :], eye * mine) * active
        bias_s[(t + 1) * BLOCK:(t + 2) * BLOCK, :] = (seen - 1.0) * 1e30

    feats = feat_s[...]
    k_s[...] = dot_nn(feats, wqkv_ref[:, width:2 * width]).astype(BF16)
    v_s[...] = dot_nn(feats, wqkv_ref[:, 2 * width:]).astype(BF16)
    kt_s[...] = dot_nt(wqkvt_ref[width:2 * width, :], feats).astype(BF16)
    vt_s[...] = dot_nt(wqkvt_ref[2 * width:, :], feats).astype(BF16)
    qt = (dot_nt(wqkvt_ref[0:width, :], feat) * (scale * math.log2(math.e))).astype(BF16)
    head_of_row = lax.broadcasted_iota(jnp.int32, (width, BLOCK), 0) // hw

    def diagonal(values, pair):
        left = jnp.where(head_of_row == 2 * pair, values, jnp.zeros_like(values))
        right = jnp.where(head_of_row == 2 * pair + 1, values, jnp.zeros_like(values))
        return jnp.concatenate([left, right], axis=1)

    qf = qt.astype(F32)
    for p in range(PAIRS):
        r = 2 * hw * p
        qbd = diagonal(qf, p).astype(BF16)
        qbd_s[p] = qbd
        bias = bias_s[...]
        scores = dot_nn(k_s[...], qbd) + jnp.concatenate([bias, bias], axis=1)
        top = jnp.max(scores, axis=0, keepdims=True)
        weights = jnp.exp2(scores - top)
        rl = 1.0 / jnp.sum(weights, axis=0, keepdims=True)
        rl_s[p] = jnp.broadcast_to(rl, (8, 2 * BLOCK))
        wb = weights.astype(BF16)
        e_s[p] = wb
        ot = dot_nn(vt_s[r:r + 2 * hw, :], wb) * rl
        att_s[r:r + hw, :] = ot[0:hw, 0:BLOCK]
        att_s[r + hw:r + 2 * hw, :] = ot[hw:2 * hw, BLOCK:]

    att_t = att_s[...]
    attended = att_t.T.astype(BF16)
    mixed = (feat.astype(F32) + dot_nn(attended, wout_ref[...])).astype(BF16)
    pre = dot_nn(mixed, wup_ref[...])
    sigma = jax.nn.sigmoid(pre)
    act = (pre * sigma).astype(BF16)
    out_ref[...] = (mixed.astype(F32) + dot_nn(act, wdown_ref[...])).astype(BF16)
    d_act = (dot_nt(cot, wdown_ref[...]) * sigma * (1.0 + pre * (1.0 - sigma))).astype(BF16)
    d_mixed = (cot.astype(F32) + dot_nt(d_act, wup_ref[...])).astype(BF16)
    d_att_t = dot_nt(wout_ref[...], d_mixed)
    gout_ref[...] += dot_tn(attended, d_mixed)
    gup_ref[...] += dot_tn(mixed, d_act)
    gdown_ref[...] += dot_tn(act, cot)

    for p in range(PAIRS):
        r = 2 * hw * p
        rl = rl_s[p][0:1, :]
        dobd32 = diagonal(d_att_t, p) * rl
        dobd = dobd32.astype(BF16)
        dobd_s[p] = dobd
        delta = jnp.sum(dobd32 * jnp.concatenate([att_t, att_t], axis=1), axis=0, keepdims=True)
        d_probs = dot_nn(v_s[...], dobd)
        ds = (e_s[p].astype(F32) * (d_probs - delta)).astype(BF16)
        ds_s[p] = ds
        dqt = dot_nn(kt_s[r:r + 2 * hw, :], ds) * scale
        dq_s[r:r + hw, :] = dqt[0:hw, 0:BLOCK]
        dq_s[r + hw:r + 2 * hw, :] = dqt[hw:2 * hw, BLOCK:]

    dq = dq_s[...].T.astype(BF16)
    gqkv_ref[:, 0:width] += dot_tn(feat, dq)
    part_ref[...] = d_mixed.astype(F32) + dot_nt(dq, wqkv_ref[:, 0:width])

    dk = dot_nt(ds_s[0], qbd_s[0])
    dv = dot_nt(e_s[0], dobd_s[0])
    for p in range(1, PAIRS):
        dk += dot_nt(ds_s[p], qbd_s[p])
        dv += dot_nt(e_s[p], dobd_s[p])
    dk = dk * math.log(2.0)
    near_ref[:, 0:width] = dk[0:BLOCK]
    near_ref[:, width:] = dv[0:BLOCK]
    dkb = dk.astype(BF16)
    dvb = dv.astype(BF16)
    for t in range(EXP):
        place = pl.multiple_of(slot_s[b * EXP + t] * BLOCK, BLOCK)
        far_ref[pl.ds(place, BLOCK), 0:width] = dkb[(t + 1) * BLOCK:(t + 2) * BLOCK]
        far_ref[pl.ds(place, BLOCK), width:] = dvb[(t + 1) * BLOCK:(t + 2) * BLOCK]
    gqkv_ref[:, width:2 * width] += dot_tn(feats, dkb)
    gqkv_ref[:, 2 * width:] += dot_tn(feats, dvb)


def run_layer(scalars, features, cot, live_col, gathered, glive_col, weights, slots):
    rows, width = features.shape
    w_qkv, w_qkv_t, w_out, w_up, w_down = weights
    hidden = w_up.shape[1]
    blocks = rows // BLOCK
    keys = TILES * BLOCK

    def by_block(cols):
        return pl.BlockSpec((BLOCK, cols), lambda b, *_: (b, 0))

    def whole(array):
        return pl.BlockSpec(array.shape, lambda b, *_: (0, 0))

    out_shape = [
        jax.ShapeDtypeStruct((rows, width), BF16),
        jax.ShapeDtypeStruct((rows, width), F32),
        jax.ShapeDtypeStruct((rows, 2 * width), F32),
        jax.ShapeDtypeStruct((slots * BLOCK, 2 * width), BF16),
        jax.ShapeDtypeStruct((width, 3 * width), F32),
        jax.ShapeDtypeStruct((width, width), F32),
        jax.ShapeDtypeStruct((width, hidden), F32),
        jax.ShapeDtypeStruct((hidden, width), F32),
    ]
    return pl.pallas_call(
        layer_kernel,
        out_shape=out_shape,
        grid_spec=pltpu.PrefetchScalarGridSpec(
            num_scalar_prefetch=4,
            grid=(blocks,),
            in_specs=[
                by_block(width), by_block(width), by_block(1),
                whole(gathered), whole(glive_col),
                whole(w_qkv), whole(w_qkv_t), whole(w_out), whole(w_up), whole(w_down),
            ],
            out_specs=[by_block(width), by_block(width), by_block(2 * width)]
            + [whole(s) for s in out_shape[3:]],
            scratch_shapes=[
                pltpu.VMEM((keys, width), BF16),
                pltpu.VMEM((keys, width), BF16),
                pltpu.VMEM((keys, width), BF16),
                pltpu.VMEM((width, keys), BF16),
                pltpu.VMEM((width, keys), BF16),
                pltpu.VMEM((keys, BLOCK), F32),
                pltpu.VMEM((PAIRS, keys, 2 * BLOCK), BF16),
                pltpu.VMEM((PAIRS, keys, 2 * BLOCK), BF16),
                pltpu.VMEM((PAIRS, width, 2 * BLOCK), BF16),
                pltpu.VMEM((PAIRS, width, 2 * BLOCK), BF16),
                pltpu.VMEM((width, BLOCK), F32),
                pltpu.VMEM((width, BLOCK), F32),
                pltpu.VMEM((PAIRS, 8, 2 * BLOCK), F32),
            ],
        ),
        compiler_params=pltpu.CompilerParams(
            dimension_semantics=("arbitrary",), vmem_limit_bytes=56 * 2**20
        ),
    )(*scalars, features, cot, live_col, gathered, glive_col, w_qkv, w_qkv_t, w_out, w_up, w_down)


def local(node_features, cotangent, w_qkv, w_out, w_up, w_down, tile_cols, tile_count, live):
    features = node_features[0]
    grad_in = cotangent[0]
    rows_dev, width = features.shape
    blocks_dev = rows_dev // BLOCK
    dom_count = lax.axis_size("dom")
    own_index = lax.axis_index("dom")
    capacity = max(2, -(-(blocks_dev * EXP) // dom_count))
    slots = dom_count * capacity
    everything = capacity == blocks_dev
    live_rows = capacity * BLOCK // width
    live_local = live[0].astype(BF16)
    table = tile_cols[0].reshape(dom_count, blocks_dev * EXP)
    my_refs = lax.dynamic_index_in_dim(table, own_index, 0, keepdims=False)

    def padded(values):
        return jnp.pad(values, ((0, 0),) * (values.ndim - 2) + ((0, EXTRA - live_rows), (0, 0)))

    if everything:
        slot = my_refs
        payload = jnp.concatenate(
            [features, padded(live_local.reshape(live_rows, width))], axis=0
        )
        got = lax.all_gather(payload, "dom", axis=0, tiled=False)
    else:
        owner_dev = table // blocks_dev
        same_owner = owner_dev[:, :, None] == owner_dev[:, None, :]
        smaller = table[:, None, :] < table[:, :, None]
        slot_rank = jnp.sum(same_owner & smaller, axis=2)
        my_rank = lax.dynamic_index_in_dim(slot_rank, own_index, 0, keepdims=False)
        slot = my_refs // blocks_dev * capacity + my_rank
        slot_ids = jnp.arange(capacity, dtype=jnp.int32)
        wanted = (slot_rank[:, :, None] == slot_ids[None, None, :]) & (owner_dev == own_index)[
            :, :, None
        ]
        local_block = table - own_index * blocks_dev
        send_index = jnp.sum(jnp.where(wanted, local_block[:, :, None], 0), axis=1)
        sent = features.reshape(blocks_dev, BLOCK, width)[send_index]
        sent_live = live_local.reshape(blocks_dev, BLOCK)[send_index]
        payload = jnp.concatenate(
            [
                sent.reshape(dom_count, capacity * BLOCK, width),
                padded(sent_live.reshape(dom_count, live_rows, width)),
            ],
            axis=1,
        )
        got = lax.all_to_all(payload, "dom", split_axis=0, concat_axis=0, tiled=True)
    stride = capacity * BLOCK + EXTRA
    glive_col = (
        got[:, capacity * BLOCK:capacity * BLOCK + live_rows, :]
        .reshape(slots * BLOCK, 1)
        .astype(F32)
    )
    row_at = slot // capacity * stride + slot % capacity * BLOCK
    own_block = own_index * blocks_dev + jnp.arange(blocks_dev * EXP, dtype=jnp.int32) // EXP
    mine = (my_refs == own_block).astype(jnp.int32)
    layer_out, part, near, far, g_qkv, g_out, g_up, g_down = run_layer(
        (row_at, slot, mine, tile_count[0]),
        features,
        grad_in,
        live[0].astype(F32).reshape(rows_dev, 1),
        got.reshape(dom_count * stride, width),
        glive_col,
        (w_qkv, w_qkv.T, w_out, w_up, w_down),
        slots,
    )
    if everything:
        summed = lax.psum_scatter(far, "dom", scatter_dimension=0, tiled=True).astype(F32)
    else:
        back = lax.all_to_all(
            far.reshape(dom_count, capacity, BLOCK, 2 * width),
            "dom",
            split_axis=0,
            concat_axis=0,
            tiled=True,
        )
        summed = (
            jnp.zeros((blocks_dev, BLOCK, 2 * width), F32)
            .at[send_index.reshape(-1)]
            .add(back.reshape(slots, BLOCK, 2 * width).astype(F32))
            .reshape(rows_dev, 2 * width)
        )
    grads = lax.psum((g_qkv, g_out, g_up, g_down), ("dom", "rep"))
    d_kv = (near + summed).astype(BF16)
    feature_grad = (part + dot_nt(d_kv, w_qkv[:, width:])).astype(BF16)
    factor = float(rows_dev * dom_count * lax.axis_size("rep")) ** (-0.5)
    return (layer_out[None], feature_grad[None]) + tuple(g * factor for g in grads)


def solution(mesh):
    return jax.shard_map(
        local,
        mesh=mesh,
        in_specs=(
            P("rep", "dom", None),
            P("rep", "dom", None),
            P(),
            P(),
            P(),
            P(),
            P("rep", None, None),
            P("rep", "dom"),
            P("rep", "dom"),
        ),
        out_specs=(P("rep", "dom", None), P("rep", "dom", None), P(), P(), P(), P()),
        check_vma=False,
    )
```

```python
import functools
import math

import jax
import jax.numpy as jnp
from jax import lax
from jax.experimental import pallas as pl
from jax.experimental.pallas import tpu as pltpu
from jax.sharding import PartitionSpec as P

HEADS = 8
BLOCK = 128
EXP = 8
TILES = EXP + 1
EXTRA = 16
PAIRS = HEADS // 2

F32 = jnp.float32
BF16 = jnp.bfloat16


def dot_nn(a, b):
    return lax.dot_general(a, b, (((1,), (0,)), ((), ())), preferred_element_type=F32)


def dot_nt(a, b):
    return lax.dot_general(a, b, (((1,), (1,)), ((), ())), preferred_element_type=F32)


def dot_tn(a, b):
    return lax.dot_general(a, b, (((0,), (0,)), ((), ())), preferred_element_type=F32)


def layer_kernel(
    factor,
    row_s, slot_s, self_s, count_s,
    feat_ref, cot_ref, live_ref, gath_ref, glive_ref,
    wqkv_ref, wqkvt_ref, wout_ref, wup_ref, wdown_ref,
    out_ref, part_ref, near_ref, far_ref, gqkv_ref, gout_ref, gup_ref, gdown_ref,
    feat_s, k_s, v_s, kt_s, vt_s, bias_s, e_s, ds_s, qbd_s, dobd_s, att_s, dq_s, rl_s,
):
    b = pl.program_id(0)
    width = feat_ref.shape[1]
    hw = width // HEADS
    scale = float(hw) ** -0.5

    @pl.when(b == 0)
    def _():
        gqkv_ref[...] = jnp.zeros_like(gqkv_ref)
        gout_ref[...] = jnp.zeros_like(gout_ref)
        gup_ref[...] = jnp.zeros_like(gup_ref)
        gdown_ref[...] = jnp.zeros_like(gdown_ref)

    eye = (
        lax.broadcasted_iota(jnp.int32, (BLOCK, BLOCK), 0)
        == lax.broadcasted_iota(jnp.int32, (BLOCK, BLOCK), 1)
    ).astype(F32)
    feat = feat_ref[...]
    cot = cot_ref[...]
    feat_s[0:BLOCK, :] = feat

    def column(ref, index):
        return jnp.sum(eye * ref[pl.ds(index, 1), :], axis=1, keepdims=True)

    bias_s[0:BLOCK, :] = (jnp.maximum(column(live_ref, b), eye) - 1.0) * 1e30
    for t in range(EXP):
        row = pl.multiple_of(row_s[b * EXP + t], 16)
        active = (t + 1 < count_s[b]).astype(F32)
        mine = self_s[b * EXP + t].astype(F32)
        feat_s[(t + 1) * BLOCK:(t + 2) * BLOCK, :] = gath_ref[pl.ds(row, BLOCK), :]
        seen = jnp.maximum(column(glive_ref, slot_s[b * EXP + t]), eye * mine) * active
        bias_s[(t + 1) * BLOCK:(t + 2) * BLOCK, :] = (seen - 1.0) * 1e30

    feats = feat_s[...]
    k_s[...] = dot_nn(feats, wqkv_ref[:, width:2 * width]).astype(BF16)
    v_s[...] = dot_nn(feats, wqkv_ref[:, 2 * width:]).astype(BF16)
    kt_s[...] = dot_nt(wqkvt_ref[width:2 * width, :], feats).astype(BF16)
    vt_s[...] = dot_nt(wqkvt_ref[2 * width:, :], feats).astype(BF16)
    qt = (dot_nt(wqkvt_ref[0:width, :], feat) * (scale * math.log2(math.e))).astype(BF16)
    head_of_row = lax.broadcasted_iota(jnp.int32, (width, BLOCK), 0) // hw

    def diagonal(values, pair):
        left = jnp.where(head_of_row == 2 * pair, values, jnp.zeros_like(values))
        right = jnp.where(head_of_row == 2 * pair + 1, values, jnp.zeros_like(values))
        return jnp.concatenate([left, right], axis=1)

    qf = qt.astype(F32)
    for p in range(PAIRS):
        r = 2 * hw * p
        qbd = diagonal(qf, p).astype(BF16)
        qbd_s[p] = qbd
        bias = bias_s[...]
        scores = dot_nn(k_s[...], qbd) + jnp.concatenate([bias, bias], axis=1)
        top = jnp.max(scores, axis=0, keepdims=True)
        weights = jnp.exp2(scores - top)
        rl = 1.0 / jnp.sum(weights, axis=0, keepdims=True)
        rl_s[p] = jnp.broadcast_to(rl, (8, 2 * BLOCK))
        wb = weights.astype(BF16)
        e_s[p] = wb
        ot = dot_nn(vt_s[r:r + 2 * hw, :], wb) * rl
        att_s[r:r + hw, :] = ot[0:hw, 0:BLOCK]
        att_s[r + hw:r + 2 * hw, :] = ot[hw:2 * hw, BLOCK:]

    att_t = att_s[...]
    attended = att_t.T.astype(BF16)
    mixed = (feat.astype(F32) + dot_nn(attended, wout_ref[...])).astype(BF16)
    pre = dot_nn(mixed, wup_ref[...])
    sigma = jax.nn.sigmoid(pre)
    act = (pre * sigma).astype(BF16)
    out_ref[...] = (mixed.astype(F32) + dot_nn(act, wdown_ref[...])).astype(BF16)
    d_act = (dot_nt(cot, wdown_ref[...]) * sigma * (1.0 + pre * (1.0 - sigma))).astype(BF16)
    d_mixed = (cot.astype(F32) + dot_nt(d_act, wup_ref[...])).astype(BF16)
    d_att_t = dot_nt(wout_ref[...], d_mixed)
    gout_ref[...] += dot_tn(attended, d_mixed)
    gup_ref[...] += dot_tn(mixed, d_act)
    gdown_ref[...] += dot_tn(act, cot)

    for p in range(PAIRS):
        r = 2 * hw * p
        rl = rl_s[p][0:1, :]
        dobd32 = diagonal(d_att_t, p) * rl
        dobd = dobd32.astype(BF16)
        dobd_s[p] = dobd
        delta = jnp.sum(dobd32 * jnp.concatenate([att_t, att_t], axis=1), axis=0, keepdims=True)
        d_probs = dot_nn(v_s[...], dobd)
        ds = (e_s[p].astype(F32) * (d_probs - delta)).astype(BF16)
        ds_s[p] = ds
        dqt = dot_nn(kt_s[r:r + 2 * hw, :], ds) * scale
        dq_s[r:r + hw, :] = dqt[0:hw, 0:BLOCK]
        dq_s[r + hw:r + 2 * hw, :] = dqt[hw:2 * hw, BLOCK:]

    dq = dq_s[...].T.astype(BF16)
    gqkv_ref[:, 0:width] += dot_tn(feat, dq)
    part_ref[...] = d_mixed.astype(F32) + dot_nt(dq, wqkv_ref[:, 0:width])

    dk = dot_nt(ds_s[0], qbd_s[0])
    dv = dot_nt(e_s[0], dobd_s[0])
    for p in range(1, PAIRS):
        dk += dot_nt(ds_s[p], qbd_s[p])
        dv += dot_nt(e_s[p], dobd_s[p])
    dk = dk * math.log(2.0)
    near_ref[:, 0:width] = dk[0:BLOCK]
    near_ref[:, width:] = dv[0:BLOCK]
    dkb = dk.astype(BF16)
    dvb = dv.astype(BF16)
    for t in range(EXP):
        place = pl.multiple_of(slot_s[b * EXP + t] * BLOCK, BLOCK)
        far_ref[pl.ds(place, BLOCK), 0:width] = dkb[(t + 1) * BLOCK:(t + 2) * BLOCK]
        far_ref[pl.ds(place, BLOCK), width:] = dvb[(t + 1) * BLOCK:(t + 2) * BLOCK]
    gqkv_ref[:, width:2 * width] += dot_tn(feats, dkb)
    gqkv_ref[:, 2 * width:] += dot_tn(feats, dvb)

    @pl.when(b == pl.num_programs(0) - 1)
    def _():
        for ref in (gqkv_ref, gout_ref, gup_ref, gdown_ref):
            ref[...] = ref[...] * factor


def run_layer(scalars, features, cot, live_rows, gathered, glive_rows, weights, slots, factor):
    rows, width = features.shape
    w_qkv, w_qkv_t, w_out, w_up, w_down = weights
    hidden = w_up.shape[1]
    blocks = rows // BLOCK
    keys = TILES * BLOCK

    def by_block(cols):
        return pl.BlockSpec((BLOCK, cols), lambda b, *_: (b, 0))

    def whole(array):
        return pl.BlockSpec(array.shape, lambda b, *_: (0, 0))

    out_shape = [
        jax.ShapeDtypeStruct((rows, width), BF16),
        jax.ShapeDtypeStruct((rows, width), F32),
        jax.ShapeDtypeStruct((rows, 2 * width), F32),
        jax.ShapeDtypeStruct((slots * BLOCK, 2 * width), BF16),
        jax.ShapeDtypeStruct((width, 3 * width), F32),
        jax.ShapeDtypeStruct((width, width), F32),
        jax.ShapeDtypeStruct((width, hidden), F32),
        jax.ShapeDtypeStruct((hidden, width), F32),
    ]
    return pl.pallas_call(
        functools.partial(layer_kernel, factor),
        out_shape=out_shape,
        grid_spec=pltpu.PrefetchScalarGridSpec(
            num_scalar_prefetch=4,
            grid=(blocks,),
            in_specs=[
                by_block(width), by_block(width), whole(live_rows),
                whole(gathered), whole(glive_rows),
                whole(w_qkv), whole(w_qkv_t), whole(w_out), whole(w_up), whole(w_down),
            ],
            out_specs=[by_block(width), by_block(width), by_block(2 * width)]
            + [whole(s) for s in out_shape[3:]],
            scratch_shapes=[
                pltpu.VMEM((keys, width), BF16),
                pltpu.VMEM((keys, width), BF16),
                pltpu.VMEM((keys, width), BF16),
                pltpu.VMEM((width, keys), BF16),
                pltpu.VMEM((width, keys), BF16),
                pltpu.VMEM((keys, BLOCK), F32),
                pltpu.VMEM((PAIRS, keys, 2 * BLOCK), BF16),
                pltpu.VMEM((PAIRS, keys, 2 * BLOCK), BF16),
                pltpu.VMEM((PAIRS, width, 2 * BLOCK), BF16),
                pltpu.VMEM((PAIRS, width, 2 * BLOCK), BF16),
                pltpu.VMEM((width, BLOCK), F32),
                pltpu.VMEM((width, BLOCK), F32),
                pltpu.VMEM((PAIRS, 8, 2 * BLOCK), F32),
            ],
        ),
        compiler_params=pltpu.CompilerParams(
            dimension_semantics=("arbitrary",), vmem_limit_bytes=56 * 2**20
        ),
    )(*scalars, features, cot, live_rows, gathered, glive_rows, w_qkv, w_qkv_t, w_out, w_up, w_down)


def local(node_features, cotangent, w_qkv, w_out, w_up, w_down, tile_cols, tile_count, live):
    features = node_features[0]
    grad_in = cotangent[0]
    rows_dev, width = features.shape
    blocks_dev = rows_dev // BLOCK
    dom_count = lax.axis_size("dom")
    own_index = lax.axis_index("dom")
    capacity = max(2, -(-(blocks_dev * EXP) // dom_count))
    slots = dom_count * capacity
    everything = capacity == blocks_dev
    packed = capacity * BLOCK // width
    live_local = live[0].astype(BF16)
    table = tile_cols[0].reshape(dom_count, blocks_dev * EXP)
    my_refs = lax.dynamic_index_in_dim(table, own_index, 0, keepdims=False)

    def padded(values):
        return jnp.pad(values, ((0, 0),) * (values.ndim - 2) + ((0, EXTRA - packed), (0, 0)))

    if everything:
        slot = my_refs
        payload = jnp.concatenate(
            [features, padded(live_local.reshape(packed, width))], axis=0
        )
        got = lax.all_gather(payload, "dom", axis=0, tiled=False)
    else:
        owner_dev = table // blocks_dev
        same_owner = owner_dev[:, :, None] == owner_dev[:, None, :]
        smaller = table[:, None, :] < table[:, :, None]
        slot_rank = jnp.sum(same_owner & smaller, axis=2)
        my_rank = lax.dynamic_index_in_dim(slot_rank, own_index, 0, keepdims=False)
        slot = my_refs // blocks_dev * capacity + my_rank
        slot_ids = jnp.arange(capacity, dtype=jnp.int32)
        wanted = (slot_rank[:, :, None] == slot_ids[None, None, :]) & (owner_dev == own_index)[
            :, :, None
        ]
        local_block = table - own_index * blocks_dev
        send_index = jnp.sum(jnp.where(wanted, local_block[:, :, None], 0), axis=1)
        sent = features.reshape(blocks_dev, BLOCK, width)[send_index]
        sent_live = live_local.reshape(blocks_dev, BLOCK)[send_index]
        payload = jnp.concatenate(
            [
                sent.reshape(dom_count, capacity * BLOCK, width),
                padded(sent_live.reshape(dom_count, packed, width)),
            ],
            axis=1,
        )
        got = lax.all_to_all(payload, "dom", split_axis=0, concat_axis=0, tiled=True)
    stride = capacity * BLOCK + EXTRA
    glive_rows = (
        got[:, capacity * BLOCK:capacity * BLOCK + packed, :]
        .reshape(slots, BLOCK)
        .astype(F32)
    )
    row_at = slot // capacity * stride + slot % capacity * BLOCK
    own_block = own_index * blocks_dev + jnp.arange(blocks_dev * EXP, dtype=jnp.int32) // EXP
    mine = (my_refs == own_block).astype(jnp.int32)
    factor = float(rows_dev * dom_count * lax.axis_size("rep")) ** (-0.5)
    layer_out, part, near, far, g_qkv, g_out, g_up, g_down = run_layer(
        (row_at, slot, mine, tile_count[0]),
        features,
        grad_in,
        live[0].astype(F32).reshape(blocks_dev, BLOCK),
        got.reshape(dom_count * stride, width),
        glive_rows,
        (w_qkv, w_qkv.T, w_out, w_up, w_down),
        slots,
        factor,
    )
    if everything:
        back = lax.all_to_all(
            far.reshape(dom_count, rows_dev, 2 * width),
            "dom",
            split_axis=0,
            concat_axis=0,
            tiled=True,
        )
        summed = jnp.sum(back.astype(F32), axis=0)
    else:
        back = lax.all_to_all(
            far.reshape(dom_count, capacity, BLOCK, 2 * width),
            "dom",
            split_axis=0,
            concat_axis=0,
            tiled=True,
        )
        summed = (
            jnp.zeros((blocks_dev, BLOCK, 2 * width), F32)
            .at[send_index.reshape(-1)]
            .add(back.reshape(slots, BLOCK, 2 * width).astype(F32))
            .reshape(rows_dev, 2 * width)
        )
    grads = lax.psum((g_qkv, g_out, g_up, g_down), ("dom", "rep"))
    d_kv = (near + summed).astype(BF16)
    feature_grad = (part + dot_nt(d_kv, w_qkv[:, width:])).astype(BF16)
    return (layer_out[None], feature_grad[None]) + tuple(grads)


def solution(mesh):
    return jax.shard_map(
        local,
        mesh=mesh,
        in_specs=(
            P("rep", "dom", None),
            P("rep", "dom", None),
            P(),
            P(),
            P(),
            P(),
            P("rep", None, None),
            P("rep", "dom"),
            P("rep", "dom"),
        ),
        out_specs=(P("rep", "dom", None), P("rep", "dom", None), P(), P(), P(), P()),
        check_vma=False,
    )
```

```python
import functools
import math

import jax
import jax.numpy as jnp
from jax import lax
from jax.experimental import pallas as pl
from jax.experimental.pallas import tpu as pltpu
from jax.sharding import PartitionSpec as P

HEADS = 8
BLOCK = 128
EXP = 8
TILES = EXP + 1
EXTRA = 16
PAIRS = HEADS // 2

F32 = jnp.float32
BF16 = jnp.bfloat16


def dot_nn(a, b):
    return lax.dot_general(a, b, (((1,), (0,)), ((), ())), preferred_element_type=F32)


def dot_nt(a, b):
    return lax.dot_general(a, b, (((1,), (1,)), ((), ())), preferred_element_type=F32)


def dot_tn(a, b):
    return lax.dot_general(a, b, (((0,), (0,)), ((), ())), preferred_element_type=F32)


def layer_kernel(
    factor,
    row_s, slot_s, self_s, count_s,
    feat_ref, cot_ref, live_ref, gath_ref, glive_ref,
    wqkv_ref, wqkvt_ref, wout_ref, wup_ref, wdown_ref,
    out_ref, part_ref, near_ref, far_ref, gqkv_ref, gout_ref, gup_ref, gdown_ref,
    feat_s, k_s, v_s, kt_s, vt_s, bias_s, e_s, ds_s, qbd_s, dobd_s, att_s, dq_s, rl_s,
):
    b = pl.program_id(0)
    width = feat_ref.shape[1]
    hw = width // HEADS
    scale = float(hw) ** -0.5

    @pl.when(b == 0)
    def _():
        gqkv_ref[...] = jnp.zeros_like(gqkv_ref)
        gout_ref[...] = jnp.zeros_like(gout_ref)
        gup_ref[...] = jnp.zeros_like(gup_ref)
        gdown_ref[...] = jnp.zeros_like(gdown_ref)

    eye = (
        lax.broadcasted_iota(jnp.int32, (BLOCK, BLOCK), 0)
        == lax.broadcasted_iota(jnp.int32, (BLOCK, BLOCK), 1)
    ).astype(F32)
    feat = feat_ref[...]
    cot = cot_ref[...]
    feat_s[0:BLOCK, :] = feat

    def column(ref, index):
        return jnp.sum(eye * ref[pl.ds(index, 1), :], axis=1, keepdims=True)

    bias_s[0:BLOCK, :] = (jnp.maximum(column(live_ref, b), eye) - 1.0) * 1e30
    for t in range(EXP):
        row = pl.multiple_of(row_s[b * EXP + t], 16)
        active = (t + 1 < count_s[b]).astype(F32)
        mine = self_s[b * EXP + t].astype(F32)
        feat_s[(t + 1) * BLOCK:(t + 2) * BLOCK, :] = gath_ref[pl.ds(row, BLOCK), :]
        seen = jnp.maximum(column(glive_ref, slot_s[b * EXP + t]), eye * mine) * active
        bias_s[(t + 1) * BLOCK:(t + 2) * BLOCK, :] = (seen - 1.0) * 1e30

    feats = feat_s[...]
    k_s[...] = dot_nn(feats, wqkv_ref[:, width:2 * width]).astype(BF16)
    v_s[...] = dot_nn(feats, wqkv_ref[:, 2 * width:]).astype(BF16)
    kt_s[...] = dot_nt(wqkvt_ref[width:2 * width, :], feats).astype(BF16)
    vt_s[...] = dot_nt(wqkvt_ref[2 * width:, :], feats).astype(BF16)
    qt = (dot_nt(wqkvt_ref[0:width, :], feat) * (scale * math.log2(math.e))).astype(BF16)
    head_of_row = lax.broadcasted_iota(jnp.int32, (width, BLOCK), 0) // hw

    def diagonal(values, pair):
        left = jnp.where(head_of_row == 2 * pair, values, jnp.zeros_like(values))
        right = jnp.where(head_of_row == 2 * pair + 1, values, jnp.zeros_like(values))
        return jnp.concatenate([left, right], axis=1)

    qf = qt.astype(F32)
    for p in range(PAIRS):
        r = 2 * hw * p
        qbd = diagonal(qf, p).astype(BF16)
        qbd_s[p] = qbd
        bias = bias_s[...]
        scores = dot_nn(k_s[...], qbd) + jnp.concatenate([bias, bias], axis=1)
        top = jnp.max(scores, axis=0, keepdims=True)
        weights = jnp.exp2(scores - top)
        rl = 1.0 / jnp.sum(weights, axis=0, keepdims=True)
        rl_s[p] = jnp.broadcast_to(rl, (8, 2 * BLOCK))
        wb = weights.astype(BF16)
        e_s[p] = wb
        ot = dot_nn(vt_s[r:r + 2 * hw, :], wb) * rl
        att_s[r:r + hw, :] = ot[0:hw, 0:BLOCK]
        att_s[r + hw:r + 2 * hw, :] = ot[hw:2 * hw, BLOCK:]

    att_t = att_s[...]
    attended = att_t.T.astype(BF16)
    mixed = (feat.astype(F32) + dot_nn(attended, wout_ref[...])).astype(BF16)
    pre = dot_nn(mixed, wup_ref[...])
    sigma = jax.nn.sigmoid(pre)
    act = (pre * sigma).astype(BF16)
    out_ref[...] = (mixed.astype(F32) + dot_nn(act, wdown_ref[...])).astype(BF16)
    d_act = (dot_nt(cot, wdown_ref[...]) * sigma * (1.0 + pre * (1.0 - sigma))).astype(BF16)
    d_mixed = (cot.astype(F32) + dot_nt(d_act, wup_ref[...])).astype(BF16)
    d_att_t = dot_nt(wout_ref[...], d_mixed)
    gout_ref[...] += dot_tn(attended, d_mixed)
    gup_ref[...] += dot_tn(mixed, d_act)
    gdown_ref[...] += dot_tn(act, cot)

    for p in range(PAIRS):
        r = 2 * hw * p
        rl = rl_s[p][0:1, :]
        dobd32 = diagonal(d_att_t, p) * rl
        dobd = dobd32.astype(BF16)
        dobd_s[p] = dobd
        delta = jnp.sum(dobd32 * jnp.concatenate([att_t, att_t], axis=1), axis=0, keepdims=True)
        d_probs = dot_nn(v_s[...], dobd)
        ds = (e_s[p].astype(F32) * (d_probs - delta)).astype(BF16)
        ds_s[p] = ds
        dqt = dot_nn(kt_s[r:r + 2 * hw, :], ds) * scale
        dq_s[r:r + hw, :] = dqt[0:hw, 0:BLOCK]
        dq_s[r + hw:r + 2 * hw, :] = dqt[hw:2 * hw, BLOCK:]

    dq = dq_s[...].T.astype(BF16)
    gqkv_ref[:, 0:width] += dot_tn(feat, dq)
    part_ref[...] = d_mixed.astype(F32) + dot_nt(dq, wqkv_ref[:, 0:width])

    dk = dot_nt(ds_s[0], qbd_s[0])
    dv = dot_nt(e_s[0], dobd_s[0])
    for p in range(1, PAIRS):
        dk += dot_nt(ds_s[p], qbd_s[p])
        dv += dot_nt(e_s[p], dobd_s[p])
    dk = dk * math.log(2.0)
    near_ref[:, 0:width] = dk[0:BLOCK]
    near_ref[:, width:] = dv[0:BLOCK]
    dkb = dk.astype(BF16)
    dvb = dv.astype(BF16)
    for t in range(EXP):
        place = pl.multiple_of(slot_s[b * EXP + t] * BLOCK, BLOCK)
        far_ref[pl.ds(place, BLOCK), 0:width] = dkb[(t + 1) * BLOCK:(t + 2) * BLOCK]
        far_ref[pl.ds(place, BLOCK), width:] = dvb[(t + 1) * BLOCK:(t + 2) * BLOCK]
    gqkv_ref[:, width:2 * width] += dot_tn(feats, dkb)
    gqkv_ref[:, 2 * width:] += dot_tn(feats, dvb)

    @pl.when(b == pl.num_programs(0) - 1)
    def _():
        for ref in (gqkv_ref, gout_ref, gup_ref, gdown_ref):
            ref[...] = ref[...] * factor


def run_layer(scalars, features, cot, live_rows, gathered, glive_rows, weights, slots, factor):
    rows, width = features.shape
    w_qkv, w_qkv_t, w_out, w_up, w_down = weights
    hidden = w_up.shape[1]
    blocks = rows // BLOCK
    keys = TILES * BLOCK

    def by_block(cols):
        return pl.BlockSpec((BLOCK, cols), lambda b, *_: (b, 0))

    def whole(array):
        return pl.BlockSpec(array.shape, lambda b, *_: (0, 0))

    out_shape = [
        jax.ShapeDtypeStruct((rows, width), BF16),
        jax.ShapeDtypeStruct((rows, width), F32),
        jax.ShapeDtypeStruct((rows, 2 * width), F32),
        jax.ShapeDtypeStruct((slots * BLOCK, 2 * width), BF16),
        jax.ShapeDtypeStruct((width, 3 * width), F32),
        jax.ShapeDtypeStruct((width, width), F32),
        jax.ShapeDtypeStruct((width, hidden), F32),
        jax.ShapeDtypeStruct((hidden, width), F32),
    ]
    return pl.pallas_call(
        functools.partial(layer_kernel, factor),
        out_shape=out_shape,
        grid_spec=pltpu.PrefetchScalarGridSpec(
            num_scalar_prefetch=4,
            grid=(blocks,),
            in_specs=[
                by_block(width), by_block(width), whole(live_rows),
                whole(gathered), whole(glive_rows),
                whole(w_qkv), whole(w_qkv_t), whole(w_out), whole(w_up), whole(w_down),
            ],
            out_specs=[by_block(width), by_block(width), by_block(2 * width)]
            + [whole(s) for s in out_shape[3:]],
            scratch_shapes=[
                pltpu.VMEM((keys, width), BF16),
                pltpu.VMEM((keys, width), BF16),
                pltpu.VMEM((keys, width), BF16),
                pltpu.VMEM((width, keys), BF16),
                pltpu.VMEM((width, keys), BF16),
                pltpu.VMEM((keys, BLOCK), F32),
                pltpu.VMEM((PAIRS, keys, 2 * BLOCK), BF16),
                pltpu.VMEM((PAIRS, keys, 2 * BLOCK), BF16),
                pltpu.VMEM((PAIRS, width, 2 * BLOCK), BF16),
                pltpu.VMEM((PAIRS, width, 2 * BLOCK), BF16),
                pltpu.VMEM((width, BLOCK), F32),
                pltpu.VMEM((width, BLOCK), F32),
                pltpu.VMEM((PAIRS, 8, 2 * BLOCK), F32),
            ],
        ),
        compiler_params=pltpu.CompilerParams(
            dimension_semantics=("arbitrary",), vmem_limit_bytes=56 * 2**20
        ),
    )(*scalars, features, cot, live_rows, gathered, glive_rows, w_qkv, w_qkv_t, w_out, w_up, w_down)


def local(node_features, cotangent, w_qkv, w_out, w_up, w_down, tile_cols, tile_count, live):
    features = node_features[0]
    grad_in = cotangent[0]
    rows_dev, width = features.shape
    blocks_dev = rows_dev // BLOCK
    dom_count = lax.axis_size("dom")
    own_index = lax.axis_index("dom")
    capacity = max(2, -(-(blocks_dev * EXP) // dom_count))
    slots = dom_count * capacity
    everything = capacity == blocks_dev
    packed = capacity * BLOCK // width
    live_local = live[0].astype(BF16)
    table = tile_cols[0].reshape(dom_count, blocks_dev * EXP)
    my_refs = lax.dynamic_index_in_dim(table, own_index, 0, keepdims=False)

    def padded(values):
        return jnp.pad(values, ((0, 0),) * (values.ndim - 2) + ((0, EXTRA - packed), (0, 0)))

    if everything:
        slot = my_refs
        payload = jnp.concatenate(
            [features, padded(live_local.reshape(packed, width))], axis=0
        )
        got = lax.all_gather(payload, "dom", axis=0, tiled=False)
    else:
        owner_dev = table // blocks_dev
        same_owner = owner_dev[:, :, None] == owner_dev[:, None, :]
        smaller = table[:, None, :] < table[:, :, None]
        slot_rank = jnp.sum(same_owner & smaller, axis=2)
        my_rank = lax.dynamic_index_in_dim(slot_rank, own_index, 0, keepdims=False)
        slot = my_refs // blocks_dev * capacity + my_rank
        slot_ids = jnp.arange(capacity, dtype=jnp.int32)
        wanted = (slot_rank[:, :, None] == slot_ids[None, None, :]) & (owner_dev == own_index)[
            :, :, None
        ]
        local_block = table - own_index * blocks_dev
        send_index = jnp.sum(jnp.where(wanted, local_block[:, :, None], 0), axis=1)
        sent = features.reshape(blocks_dev, BLOCK, width)[send_index]
        sent_live = live_local.reshape(blocks_dev, BLOCK)[send_index]
        payload = jnp.concatenate(
            [
                sent.reshape(dom_count, capacity * BLOCK, width),
                padded(sent_live.reshape(dom_count, packed, width)),
            ],
            axis=1,
        )
        got = lax.all_to_all(payload, "dom", split_axis=0, concat_axis=0, tiled=True)
    stride = capacity * BLOCK + EXTRA
    glive_rows = (
        got[:, capacity * BLOCK:capacity * BLOCK + packed, :]
        .reshape(slots, BLOCK)
        .astype(F32)
    )
    row_at = slot // capacity * stride + slot % capacity * BLOCK
    own_block = own_index * blocks_dev + jnp.arange(blocks_dev * EXP, dtype=jnp.int32) // EXP
    mine = (my_refs == own_block).astype(jnp.int32)
    factor = float(rows_dev * dom_count * lax.axis_size("rep")) ** (-0.5)
    layer_out, part, near, far, g_qkv, g_out, g_up, g_down = run_layer(
        (row_at, slot, mine, tile_count[0]),
        features,
        grad_in,
        live[0].astype(F32).reshape(blocks_dev, BLOCK),
        got.reshape(dom_count * stride, width),
        glive_rows,
        (w_qkv, w_qkv.T, w_out, w_up, w_down),
        slots,
        factor,
    )
    if everything:
        back = lax.all_to_all(
            far.reshape(dom_count, rows_dev, 2 * width),
            "dom",
            split_axis=0,
            concat_axis=0,
            tiled=True,
        )
        summed = jnp.sum(back.astype(F32), axis=0)
    else:
        back = lax.all_to_all(
            far.reshape(dom_count, capacity, BLOCK, 2 * width),
            "dom",
            split_axis=0,
            concat_axis=0,
            tiled=True,
        )
        summed = (
            jnp.zeros((blocks_dev, BLOCK, 2 * width), F32)
            .at[send_index.reshape(-1)]
            .add(back.reshape(slots, BLOCK, 2 * width).astype(F32))
            .reshape(rows_dev, 2 * width)
        )
    grads = lax.psum(
        tuple(g.astype(BF16) for g in (g_qkv, g_out, g_up, g_down)), ("dom", "rep")
    )
    d_kv = (near + summed).astype(BF16)
    feature_grad = (part + dot_nt(d_kv, w_qkv[:, width:])).astype(BF16)
    return (layer_out[None], feature_grad[None]) + tuple(g.astype(F32) for g in grads)


def solution(mesh):
    return jax.shard_map(
        local,
        mesh=mesh,
        in_specs=(
            P("rep", "dom", None),
            P("rep", "dom", None),
            P(),
            P(),
            P(),
            P(),
            P("rep", None, None),
            P("rep", "dom"),
            P("rep", "dom"),
        ),
        out_specs=(P("rep", "dom", None), P("rep", "dom", None), P(), P(), P(), P()),
        check_vma=False,
    )
```
